32 devices in a mesh: node: 8 (over z, x), feat: 4 (over y, core).
Axes of the slice: x: 2, y: 2, z: 4, core: 2. Of those that a mesh axis runs over, the one named last changes fastest.
Arguments:
- out_grad: bfloat16 [256, 65536], P('feat', 'node'), may hold values from -6 to 6
- pre_act: bfloat16 [256, 65536], P('feat', 'node'), may hold values from -6 to 6
- in_act: bfloat16 [256, 65536], P(None, ('node', 'feat')), may hold values from -6 to 6
- weight: bfloat16 [256, 256], replicated, may hold values from -0.375 to 0.375
- tiles: bfloat16 [512, 24, 128, 128], P('node'), may hold values from -0.4375 to 0.4375
- indices: int32 [512, 24], P('node'), may hold values from 0 to 511, as said below
- counts: int32 [512], P('node'), may hold values from 1 to 24, as said below
Outputs:
- in_grad: bfloat16 [256, 65536], P(None, ('node', 'feat'))
- weight_grad: float32 [256, 256], replicated
The draws below stay inside these ranges and needn't reach their ends.
Inputs may be any that keep to these rules, and one draw needn't show every extreme that they name: `indices`: the 24 column blocks named by one row block are distinct; slots at or after the row block's count are ignored. Each node device has a cap between 2 and 24, and its row blocks' counts are at most that cap, except for one row block in the whole graph whose count is 24.
All inputs are finite; a program needn't handle non-finite values.
Results may differ from the reference program's by a relative error of at most 0.012.
Values may be sent and summed in bfloat16 or wider, within the bound.
A program may use at most 192 MiB of HBM per device.

```python
import jax
import jax.numpy as jnp
from jax import lax

HID = 256
BLK = 128
KMAX = 24
RB_DEV = 64
NRB = 512
NODES = 65536


def draw_indices(key, part):
    keys = jax.random.split(key, NRB)

    def one_row(row_key):
        return jax.random.permutation(row_key, NRB)[:KMAX].astype(jnp.int32)
    return jax.vmap(one_row)(keys)


def draw_counts(key, part):
    key_cap = jax.random.fold_in(key, 11)
    key_each = jax.random.fold_in(key, 23)
    key_where = jax.random.fold_in(key, 37)
    groups = NRB // RB_DEV
    caps = jax.random.randint(key_cap, (groups,), 2, KMAX + 1).astype(jnp.int32)
    caps_rows = jnp.repeat(caps, RB_DEV)
    counts = jax.random.randint(key_each, (NRB,), 1, caps_rows + 1).astype(jnp.int32)
    where_full = jax.random.randint(key_where, (), 0, NRB)
    positions = jnp.arange(NRB, dtype=jnp.int32)
    return jnp.where(positions == where_full, KMAX, counts).astype(jnp.int32)


def level_of(own_key, shape, shards, smallest, top_value):
    gain = 1.0
    for dim, blocks in shards:
        steps = jax.random.uniform(jax.random.fold_in(jax.random.fold_in(own_key, 6), dim), (blocks,), jnp.float32, smallest / len(shards), top_value / len(shards))
        gain = gain * jnp.repeat(jnp.exp(steps), shape[dim] // blocks).reshape((-1,) + (1,) * (len(shape) - 1 - dim))
    return gain


def centred(own_key, dims, spread, reach, shards=(), held_as=jnp.bfloat16):
    drawn = jax.random.normal(own_key, dims, jnp.float32) * spread
    if len(shards) > 0:
        drawn = level_of(own_key, dims, shards, -0.22, 0.18) * drawn
    return jnp.clip(drawn, min=-reach, max=reach).astype(held_as)


def setup_inputs(seed: int = 0) -> dict:
    key_list = jax.random.split(jax.random.key(seed), 8)
    return {
        "out_grad": centred(key_list[0], (HID, NODES), 1.0, 6.0, ((0, 4), (1, 8))),
        "pre_act": centred(key_list[1], (HID, NODES), 1.0, 6.0, ((0, 4), (1, 8))),
        "in_act": centred(key_list[2], (HID, NODES), 1.0, 6.0, ((1, 32),)),
        "weight": centred(key_list[3], (HID, HID), HID ** -0.5, 0.375),
        "tiles": centred(key_list[4], (NRB, KMAX, BLK, BLK), ((BLK * KMAX / 2.5) ** -0.5), 0.4375, ((0, 8),)),
        "indices": draw_indices(jax.random.fold_in(key_list[7], 71), 0),
        "counts": draw_counts(jax.random.fold_in(key_list[7], 71), 0),
    }


def reference(out_grad, pre_act, in_act, weight, tiles, indices, counts):
    grad_pre = jnp.where(pre_act > 0, out_grad, jnp.zeros_like(out_grad))
    blocks = grad_pre.reshape(HID, NRB, BLK)
    slots = jnp.arange(KMAX, dtype=jnp.int32)

    def one_block(items):
        tile, index_row, count = items
        picked = jnp.take(blocks, index_row.astype(jnp.int32), axis=1).astype(jnp.float32)
        live = (slots < count).astype(jnp.float32)
        picked = picked * live[None, :, None]
        return jnp.einsum("fkc,kic->fi", picked, tile.astype(jnp.float32))

    summed = lax.map(one_block, (tiles, indices, counts))
    aggregated = summed.transpose(1, 0, 2).reshape(HID, NODES).astype(jnp.bfloat16)
    in_grad = jnp.dot(weight, aggregated, preferred_element_type=jnp.float32).astype(jnp.bfloat16)
    scale = float(NODES) ** -0.5
    weight_grad = lax.dot_general(in_act, aggregated, (((1,), (1,)), ((), ())), preferred_element_type=jnp.float32) * scale
    return in_grad, weight_grad
```

```python
import functools

import jax
import jax.numpy as jnp
from jax import lax
from jax.experimental import pallas as pl
from jax.experimental.pallas import tpu as pltpu
from jax.sharding import PartitionSpec as P

MESH = pl.DeviceIdType.MESH
ROWS = 16
GROUP = 4
DEPTH = 8


def gather_kernel(
    n, m, width, grad_ref, act_ref, in_ref, out_ref, acts_ref,
    own, send_sem, recv_sem, local_sem, in_send, in_recv, in_local,
):
    me = lax.axis_index("node")
    mine = lax.axis_index("feat")
    height = n // width
    z, x = me // width, me % width
    pieces = own.shape[0]
    has = (z > 0, z < height - 1, x > 0, x < width - 1)
    there = (me - width, me + width, me - 1, me + 1)
    over = pieces // 2 if width == 2 and height % 2 == 0 else 0
    mate = z + 1 - 2 * (z % 2)

    barrier = pltpu.get_barrier_semaphore()
    for d in range(4):
        @pl.when(has[d])
        def _():
            pl.semaphore_signal(barrier, inc=1, device_id={"node": there[d]}, device_id_type=MESH)
    for step in range(1, m):
        pl.semaphore_signal(
            barrier, inc=1, device_id={"feat": lax.rem(mine + step, m)}, device_id_type=MESH
        )
    peers = sum(jnp.where(h, 1, 0) for h in has) + (m - 1)
    pl.semaphore_wait(barrier, peers)

    def spread(step):
        return pltpu.make_async_remote_copy(
            src_ref=in_ref,
            dst_ref=acts_ref.at[mine],
            send_sem=in_send.at[step],
            recv_sem=in_recv.at[step],
            device_id={"feat": lax.rem(mine + step, m)},
            device_id_type=MESH,
        )

    def copy(block, c, d, src):
        return pltpu.make_async_remote_copy(
            src_ref=src,
            dst_ref=out_ref.at[block, c],
            send_sem=send_sem.at[d, block, c],
            recv_sem=recv_sem.at[block, c],
            device_id={"node": there[d]},
            device_id_type=MESH,
        )

    def send(block, c, d, src):
        @pl.when(has[d])
        def _():
            copy(block, c, d, src).start()

    def arrived(block, c):
        copy(block, c, 0, out_ref.at[block, c]).wait_recv()

    def keep(c):
        return pltpu.make_async_copy(own.at[c], out_ref.at[me, c], local_sem.at[c])

    @pl.loop(0, pieces)
    def _(c):
        own[c] = jnp.where(act_ref[c] > 0, grad_ref[c], jnp.zeros_like(grad_ref[c]))
        for d in range(4):
            send(me, c, d, own.at[c])
        keep(c).start()

    own_in = pltpu.make_async_copy(in_ref, acts_ref.at[mine], in_local)
    own_in.start()
    for step in range(1, m):
        spread(step).start()

    @pl.loop(1, height)
    def _(t):
        @pl.loop(0, pieces)
        def _(c):
            for zz, onward in ((z + t, 0), (z - t, 1)):
                @pl.when((zz >= 0) & (zz < height))
                def _():
                    block = zz * width + x
                    arrived(block, c)
                    send(block, c, onward, out_ref.at[block, c])

                    @pl.when((zz != mate) | (c >= over))
                    def _():
                        for d in (2, 3):
                            send(block, c, d, out_ref.at[block, c])

            if over:
                @pl.when((t == 1) & (c < over))
                def _():
                    block = z * width + 1 - x
                    arrived(block, c)
                    for d in range(2):
                        @pl.when(z % 2 == 1 - d)
                        def _():
                            send(block, c, d, out_ref.at[block, c])

    @pl.loop(1, width)
    def _(s):
        @pl.loop(0, height)
        def _(zz):
            @pl.loop(0, pieces)
            def _(c):
                for xx, onward in ((x + s, 2), (x - s, 3)):
                    @pl.when((xx >= 0) & (xx < width) & ((zz != z) | (c >= over)))
                    def _():
                        block = zz * width + xx
                        arrived(block, c)
                        send(block, c, onward, out_ref.at[block, c])

    @pl.loop(0, n)
    def _(block):
        zz, xx = block // width, block % width

        @pl.loop(0, pieces)
        def _(c):
            direct = (zz != mate) | (c >= over)
            handed = (xx != x) & (zz == z) & (c < over)
            sent = (
                ((xx == x) & (zz >= z)) | (handed & (z % 2 == 1)),
                ((xx == x) & (zz <= z)) | (handed & (z % 2 == 0)),
                (xx >= x) & direct,
                (xx <= x) & direct,
            )
            for d in range(4):
                @pl.when(has[d] & sent[d])
                def _():
                    copy(block, c, d, out_ref.at[block, c]).wait_send()

    @pl.loop(0, pieces)
    def _(c):
        keep(c).wait()

    own_in.wait()
    for step in range(1, m):
        spread(step).wait()


def gather(n, m, grad, act, acts):
    feats, nodes = grad.shape
    width = 2 ** ((n.bit_length() - 1) // 2)
    rows = min(ROWS, feats)
    shape = (feats // rows, rows, nodes)
    pieces = shape[0]
    return pl.pallas_call(
        functools.partial(gather_kernel, n, m, width),
        out_shape=(
            jax.ShapeDtypeStruct((n, *shape), grad.dtype),
            jax.ShapeDtypeStruct((m, *acts.shape), acts.dtype),
        ),
        in_specs=[pl.BlockSpec(memory_space=pltpu.VMEM)] * 2 + [pl.BlockSpec(memory_space=pl.ANY)],
        out_specs=(pl.BlockSpec(memory_space=pl.ANY),) * 2,
        scratch_shapes=[
            pltpu.VMEM(shape, grad.dtype),
            pltpu.SemaphoreType.DMA((4, n, pieces)),
            pltpu.SemaphoreType.DMA((n, pieces)),
            pltpu.SemaphoreType.DMA((pieces,)),
            pltpu.SemaphoreType.DMA((m,)),
            pltpu.SemaphoreType.DMA((m,)),
            pltpu.SemaphoreType.DMA,
        ],
        compiler_params=pltpu.CompilerParams(
            collective_id=0, has_side_effects=True, vmem_limit_bytes=32 * 2**20
        ),
    )(grad.reshape(shape), act.reshape(shape), acts)


def sparse_kernel(index_ref, count_ref, whole_ref, tiles_ref, out_ref, held, sem):
    rows, slots, size, _ = tiles_ref.shape
    _, pieces, high, nodes = whole_ref.shape
    per_owner = nodes // size
    feats = pieces * high
    groups = slots // GROUP

    def copy(r, j):
        part = pl.ds(j * GROUP, GROUP)
        at = lax.rem(r, DEPTH)
        return pltpu.make_async_copy(tiles_ref.at[r, part], held.at[at, part], sem.at[at, j])

    def fetch(r):
        for j in range(groups):
            @pl.when(j * GROUP < count_ref[r])
            def _():
                copy(r, j).start()

    def picked(r, k, count):
        block = index_ref[r, k]
        owner = lax.div(block, per_owner)
        start = pl.multiple_of(lax.rem(block, per_owner) * size, size)
        got = whole_ref[owner, :, :, pl.ds(start, size)].reshape(feats, size)
        return jnp.where(k < count, got, jnp.zeros_like(got))

    @pl.loop(0, min(DEPTH - 1, rows))
    def _(r):
        fetch(r)

    @pl.loop(0, rows)
    def _(r):
        @pl.when(r + DEPTH - 1 < rows)
        def _():
            fetch(r + DEPTH - 1)

        count = count_ref[r]
        at = lax.rem(r, DEPTH)
        used = lax.div(count + GROUP - 1, GROUP)
        for b in range(1, groups + 1):
            @pl.when(used == b)
            def _():
                for j in range(b):
                    copy(r, j).wait()
                total = None
                for k in range(0, b * GROUP, 2):
                    left = jnp.concatenate(
                        [picked(r, k, count), picked(r, k + 1, count)], axis=1
                    )
                    right = jnp.concatenate([held[at, k], held[at, k + 1]], axis=1)
                    term = lax.dot_general(
                        left, right, (((1,), (1,)), ((), ())), preferred_element_type=jnp.float32
                    )
                    total = term if total is None else total + term
                share = rows // out_ref.shape[0]
                start = pl.multiple_of(lax.rem(r, share) * size, size)
                out_ref[lax.div(r, share), :, pl.ds(start, size)] = total.astype(out_ref.dtype)


def sparse(m, indices, counts, whole, tiles):
    rows, slots, size, _ = tiles.shape
    feats = whole.shape[1] * whole.shape[2]
    smem = pl.BlockSpec(memory_space=pltpu.SMEM)
    vmem = pl.BlockSpec(memory_space=pltpu.VMEM)
    return pl.pallas_call(
        sparse_kernel,
        out_shape=jax.ShapeDtypeStruct((m, feats, rows * size // m), whole.dtype),
        in_specs=[smem, smem, vmem, pl.BlockSpec(memory_space=pl.ANY)],
        out_specs=vmem,
        scratch_shapes=[
            pltpu.VMEM((DEPTH, slots, size, size), tiles.dtype),
            pltpu.SemaphoreType.DMA((DEPTH, slots // GROUP)),
        ],
        compiler_params=pltpu.CompilerParams(vmem_limit_bytes=48 * 2**20),
    )(indices, counts, whole, tiles)


def finish_kernel(
    n, m, scale, agg_ref, acts_ref, weight_ref, grad_ref, wgrad_ref,
    rows, parts, taken, node_part, agg_send, agg_recv, part_send, part_recv,
    sum_send, sum_recv, all_send, all_recv,
):
    node, feat = lax.axis_index("node"), lax.axis_index("feat")
    feats, share = agg_ref.shape[1:]
    high = parts.shape[1]

    barrier = pltpu.get_barrier_semaphore()
    for step in range(1, m):
        pl.semaphore_signal(
            barrier, inc=1, device_id={"feat": lax.rem(feat + step, m)}, device_id_type=MESH
        )

    @pl.loop(1, n)
    def _(step):
        pl.semaphore_signal(
            barrier, inc=1, device_id={"node": lax.rem(node + step, n)}, device_id_type=MESH
        )

    pl.semaphore_wait(barrier, m + n - 2)

    def agg_copy(step):
        to = lax.rem(feat + step, m)
        return pltpu.make_async_remote_copy(
            src_ref=agg_ref.at[to],
            dst_ref=rows.at[feat],
            send_sem=agg_send.at[step],
            recv_sem=agg_recv.at[step],
            device_id={"feat": to},
            device_id_type=MESH,
        )

    def part_copy(step):
        to = lax.rem(node + step, n)
        return pltpu.make_async_remote_copy(
            src_ref=parts.at[to],
            dst_ref=taken.at[node],
            send_sem=part_send.at[step],
            recv_sem=part_recv.at[step],
            device_id={"node": to},
            device_id_type=MESH,
        )

    def sum_copy(step):
        return pltpu.make_async_remote_copy(
            src_ref=node_part,
            dst_ref=wgrad_ref.at[feat, node],
            send_sem=sum_send.at[step],
            recv_sem=sum_recv.at[step],
            device_id={"node": lax.rem(node + step, n)},
            device_id_type=MESH,
        )

    def all_copy(step):
        return pltpu.make_async_remote_copy(
            src_ref=wgrad_ref.at[feat],
            dst_ref=wgrad_ref.at[feat],
            send_sem=all_send.at[step],
            recv_sem=all_recv.at[step],
            device_id={"feat": lax.rem(feat + step, m)},
            device_id_type=MESH,
        )

    for step in range(1, m):
        agg_copy(step).start()
    rows[feat] = agg_ref[feat]

    total = None
    for q in range(m):
        term = lax.dot_general(
            agg_ref[q], acts_ref[q], (((1,), (1,)), ((), ())), preferred_element_type=jnp.float32
        )
        total = term if total is None else total + term
    total = total * scale
    for i in range(n):
        parts[i] = total[i * high : (i + 1) * high]
    taken[node] = parts[node]

    @pl.loop(1, n)
    def _(step):
        part_copy(step).start()

    @pl.loop(1, n)
    def _(step):
        part_copy(step).wait()

    node_part[...] = jnp.sum(taken[...], axis=0)
    wgrad_ref[feat, node] = node_part[...]

    @pl.loop(1, n)
    def _(step):
        sum_copy(step).start()

    @pl.loop(1, n)
    def _(step):
        sum_copy(step).wait()

    for step in range(1, m):
        all_copy(step).start()
    for step in range(1, m):
        agg_copy(step).wait()

    wide = min(512, share)

    @pl.loop(0, share // wide)
    def _(i):
        at = pl.ds(pl.multiple_of(i * wide, wide), wide)
        right = rows[:, :, at].reshape(m * feats, wide)
        grad_ref[:, at] = jnp.dot(
            weight_ref[...], right, preferred_element_type=jnp.float32
        ).astype(grad_ref.dtype)

    for step in range(1, m):
        all_copy(step).wait()


def finish(n, m, scale, aggregated, acts, weight):
    _, feats, share = aggregated.shape
    high, wide = feats // n, acts.shape[1]
    dma = pltpu.SemaphoreType.DMA
    return pl.pallas_call(
        functools.partial(finish_kernel, n, m, scale),
        out_shape=(
            jax.ShapeDtypeStruct((weight.shape[0], share), aggregated.dtype),
            jax.ShapeDtypeStruct((m, n, high, wide), jnp.float32),
        ),
        in_specs=[pl.BlockSpec(memory_space=pltpu.VMEM)] * 3,
        out_specs=(pl.BlockSpec(memory_space=pltpu.VMEM),) * 2,
        scratch_shapes=[
            pltpu.VMEM((m, feats, share), aggregated.dtype),
            pltpu.VMEM((n, high, wide), jnp.float32),
            pltpu.VMEM((n, high, wide), jnp.float32),
            pltpu.VMEM((high, wide), jnp.float32),
            dma((m,)), dma((m,)), dma((n,)), dma((n,)), dma((n,)), dma((n,)), dma((m,)), dma((m,)),
        ],
        compiler_params=pltpu.CompilerParams(
            collective_id=1, has_side_effects=True, vmem_limit_bytes=48 * 2**20
        ),
    )(aggregated, acts, weight)


def per_device(nodes_n, feats_n, out_grad, pre_act, in_act, weight, tiles, indices, counts):
    whole, acts = gather(nodes_n, feats_n, out_grad, pre_act, in_act)
    aggregated = sparse(feats_n, indices, counts, whole, tiles)
    scale = float(nodes_n * out_grad.shape[1]) ** (-0.5)
    in_grad, turned = finish(nodes_n, feats_n, scale, aggregated, acts, weight)
    high, wide = weight.shape
    return in_grad, turned.reshape(wide, high).T


def solution(mesh):
    in_specs = (
        P("feat", "node"),
        P("feat", "node"),
        P(None, ("node", "feat")),
        P(),
        P("node", None, None, None),
        P("node", None),
        P("node"),
    )
    out_specs = (P(None, ("node", "feat")), P())
    return jax.shard_map(
        functools.partial(per_device, mesh.shape["node"], mesh.shape["feat"]),
        mesh=mesh,
        in_specs=in_specs,
        out_specs=out_specs,
        check_vma=False,
    )
```
